512 devices in a mesh: dp: 16 (over z, y_hi), ep: 32 (over y_lo, x, core).
Axes of the slice: x: 4, y: 8 (y_hi: 2, y_lo: 4; y = y_hi * 4 + y_lo), z: 8, core: 2. Of those that a mesh axis runs over, the one named last changes fastest.
Arguments:
- tokens: bfloat16 [16384, 2048], P(('dp', 'ep')), may hold values from -6 to 6
- grad_out: bfloat16 [16384, 2048], P(('dp', 'ep')), may hold values from -6 to 6
- expert_ids: int32 [16384, 2], P(('dp', 'ep')), may hold values from 0 to 7, all different within a row; in each aligned block of 32 rows (0 to 31, 32 to 63, ...) at most 9 rows name the same one
- combine: float32 [16384, 2], P(('dp', 'ep')), may hold values from 0.2 to 1
- w_gate: bfloat16 [32, 2048, 768], P('ep', 'dp'), may hold values from -0.125 to 0.125
- w_up: bfloat16 [32, 2048, 768], P('ep', 'dp'), may hold values from -0.125 to 0.125
- w_down: bfloat16 [32, 768, 2048], P('ep', None, 'dp'), may hold values from -0.109375 to 0.109375
Outputs:
- layer_out: bfloat16 [16384, 2048], P(('dp', 'ep'))
- grad_tokens: bfloat16 [16384, 2048], P(('dp', 'ep'))
- grad_gate: bfloat16 [32, 2048, 768], P('ep', 'dp')
The draws below stay inside these ranges and needn't reach their ends.
Inputs may be any that keep to these rules, and one draw needn't show every extreme that they name: `expert_ids`: in each aligned block of 32 rows (the rows of one device) no expert is named by more than 9 rows, a bound that some block reaches; the two ids of a row differ.
All inputs are finite; a program needn't handle non-finite values.
Results may differ from the reference program's by a relative error of at most 0.02.
Values may be sent and summed in bfloat16 or wider, within the bound.
No kernel may reach another device: no remote copies, remote signals or barrier semaphores. Data moves between devices by JAX's collectives and lax.ppermute only.
A program may use at most 64 MiB of HBM per device.

```python
import math
import jax
import jax.numpy as jnp
import numpy as np

D = 2048
EXPERTS = 8
HID_DEV = 768
TOK_DEV = 32
CAP = 9
SHARDS = 32
TOKENS = 16384
N_DP = 16
N_EP = 32


def levels(key, shape, split, low, high):
    def one(dim, parts):
        draws = jax.random.uniform(jax.random.fold_in(jax.random.fold_in(key, 6), dim), (parts,), jnp.float32, low / len(split), high / len(split))
        return jnp.repeat(jnp.exp(draws), shape[dim] // parts).reshape((-1,) + (1,) * (len(shape) - dim - 1))

    gain = one(*split[0])
    for cut in split[1:]:
        gain = gain * one(*cut)
    return gain


def shared_out(stream_key, own, number, rows, number_of, top, bound, lean):
    ranking = jax.random.permutation(stream_key, number_of)
    heavy_load, usual = load_shares(number_of, rows * top, bound, lean, True), load_shares(number_of, rows * top, bound, lean, False)
    places = jnp.arange(number_of)

    def named(lengths, turn):
        used = int((lengths > 0).sum())
        fixed = max(1, used // 4)
        passed = fixed + (places - fixed + turn * (used - fixed)) % max(1, number_of - fixed)
        return jnp.zeros((number_of,), jnp.int32).at[ranking[jnp.where(places < fixed, places, passed)]].set(jnp.asarray(lengths, jnp.int32))

    lengths = jnp.where(number % 4 == 0, named(heavy_load, number // 4), named(usual, number - number // 4 - 1))
    mixed = jax.random.permutation(jax.random.fold_in(own, 3), number_of)
    donor, receiver = mixed[0:number_of // 2 * 2:2], mixed[1:number_of // 2 * 2:2]
    margin = jnp.minimum(lengths[donor] - 1, bound - lengths[receiver]) // 2
    margin = jnp.where((donor == ranking[0]) | (receiver == ranking[0]) | (lengths[receiver] == 0), 0, jnp.maximum(margin, 0))
    passed = jax.random.randint(jax.random.fold_in(own, 4), (number_of // 2,), 0, 1 << 20) % (margin + 1)
    lengths = lengths.at[donor].add(-passed).at[receiver].add(passed)
    members = jnp.searchsorted(jnp.cumsum(lengths), jnp.arange(rows * top), side="right").astype(jnp.int32)
    listing = members.reshape(top, rows).T
    listing = listing[jax.random.permutation(jax.random.fold_in(own, 1), rows)]
    turn = jax.random.randint(jax.random.fold_in(own, 2), (rows, 1), 0, top)
    return jnp.take_along_axis(listing, (jnp.arange(top)[None, :] + turn) % top, axis=1)


def load_shares(count, total, limit, skew, full):
    portions = [(1 << 20) // math.isqrt(grade ** skew) + 1 for grade in range(1, count + 1)]
    largest = limit if full else min(limit, max(-(-total // count), total * portions[0] // sum(portions)))
    least = 1 if total - largest >= count - 1 else 0
    counts, surplus = [largest] + [least] * (count - 1), total - largest - least * (count - 1)
    while surplus > 0:
        candidates = [i for i in range(1, count) if counts[i] < largest] or [i for i in range(1, count) if counts[i] < limit]
        mass, budget = sum([portions[i] for i in candidates]), surplus
        for i in candidates:
            more = min(limit - counts[i], max(1, budget * portions[i] // mass), surplus)
            counts[i] = counts[i] + more
            surplus = surplus - more
    return np.array(counts)


def normal_values(rng, shape, deviation, bound, pieces=(), kind=jnp.bfloat16):
    values = deviation * jax.random.normal(rng, shape, jnp.float32)
    if pieces:
        values = values * levels(rng, shape, pieces, -0.22, 0.18)
    return jnp.clip(values, -bound, bound).astype(kind)


def setup_inputs(seed: int = 0) -> dict:
    seeds = jax.random.split(jax.random.key(seed), 8)
    tokens = normal_values(seeds[0], (TOKENS, D), 1.0, 6.0, ((0, 512),))
    grad_out = normal_values(seeds[1], (TOKENS, D), 1.0, 6.0, ((0, 512),))
    expert_ids_keys = jax.random.split(jax.random.fold_in(seeds[2], 1), TOKENS // TOK_DEV)
    expert_ids_turns = jax.random.permutation(jax.random.fold_in(seeds[2], 3), TOKENS // TOK_DEV)
    expert_ids = jax.vmap(lambda own, number: shared_out(jax.random.fold_in(seeds[2], 2), own, number, TOK_DEV, EXPERTS, 2, CAP, 1))(expert_ids_keys, expert_ids_turns).reshape((TOKENS, 2))
    combine = jnp.clip(0.2 + 0.8 * jax.random.uniform(seeds[3], (TOKENS, 2), jnp.float32) ** levels(seeds[3], (TOKENS, 2), ((0, 512),), -0.2, 0.2), 0.2, 1.0)
    w_gate = normal_values(seeds[4], (SHARDS, D, HID_DEV), D ** -0.5, 0.125, ((0, 32), (1, 16)))
    w_up = normal_values(seeds[5], (SHARDS, D, HID_DEV), D ** -0.5, 0.125, ((0, 32), (1, 16)))
    w_down = normal_values(seeds[6], (SHARDS, HID_DEV, D), (HID_DEV * N_EP // EXPERTS) ** -0.5, 0.109375, ((0, 32), (2, 16)))
    return dict(tokens=tokens, grad_out=grad_out, expert_ids=expert_ids, combine=combine, w_gate=w_gate, w_up=w_up, w_down=w_down)


def reference(tokens, grad_out, expert_ids, combine, w_gate, w_up, w_down):
    share_count = N_EP // EXPERTS
    block_count = N_DP * N_EP
    paired_ids = expert_ids.reshape(block_count, TOK_DEV * 2)
    one_hot = (paired_ids[:, :, None] == jnp.arange(EXPERTS, dtype=jnp.int32)[None, None, :]).astype(jnp.int32)
    earlier_count = jnp.cumsum(one_hot, axis=1) - one_hot
    position = jnp.sum(earlier_count * one_hot, axis=2)
    target = (paired_ids * CAP + position).astype(jnp.int32)
    entries = jnp.broadcast_to(jnp.arange(TOK_DEV * 2, dtype=jnp.int32)[None, :], (block_count, TOK_DEV * 2))
    block_index = jnp.broadcast_to(jnp.arange(block_count, dtype=jnp.int32)[:, None], (block_count, TOK_DEV * 2))
    slot_table = jnp.full((block_count, EXPERTS * CAP), -1, jnp.int32).at[block_index, target].set(entries)
    grad_sum = jnp.zeros((TOKENS, D), jnp.float32)
    out_sum = jnp.zeros((TOKENS, D), jnp.float32)
    gate_list = []
    block_start = jnp.repeat(jnp.arange(block_count, dtype=jnp.int32) * TOK_DEV, CAP)
    for expert in range(EXPERTS):
        chosen = slot_table[:, expert * CAP:(expert + 1) * CAP].reshape(-1)
        is_used = chosen >= 0
        safe_pair = jnp.where(is_used, chosen, 0)
        row_index = (block_start + safe_pair // 2).astype(jnp.int32)
        choice_index = (safe_pair % 2).astype(jnp.int32)
        used_mask = is_used[:, None]
        expert_in = jnp.where(used_mask, tokens[row_index], jnp.zeros((), jnp.bfloat16)).astype(jnp.bfloat16)
        router = combine[row_index, choice_index]
        expert_grad = jnp.where(used_mask, router[:, None] * grad_out[row_index].astype(jnp.float32), 0.0).astype(jnp.bfloat16)
        gate_full = jnp.concatenate([w_gate[expert * share_count + piece] for piece in range(share_count)], axis=1)
        up_full = jnp.concatenate([w_up[expert * share_count + piece] for piece in range(share_count)], axis=1)
        down_full = jnp.concatenate([w_down[expert * share_count + piece] for piece in range(share_count)], axis=0)
        gate_pre = jnp.dot(expert_in, gate_full, preferred_element_type=jnp.float32)
        up_pre = jnp.dot(expert_in, up_full, preferred_element_type=jnp.float32)
        grad_hidden = jnp.dot(expert_grad, down_full.T, preferred_element_type=jnp.float32)
        sigma = jax.nn.sigmoid(gate_pre)
        hidden_act = (gate_pre * sigma * up_pre).astype(jnp.bfloat16)
        grad_upper = (grad_hidden * gate_pre * sigma).astype(jnp.bfloat16)
        grad_gated = (grad_hidden * up_pre * sigma * (1.0 + gate_pre * (1.0 - sigma))).astype(jnp.bfloat16)
        grouped_in = expert_in.reshape(N_DP, N_EP * CAP, D).astype(jnp.float32)
        grouped_gate = grad_gated.reshape(N_DP, N_EP * CAP, -1).astype(jnp.float32)
        gate_terms = jnp.einsum("grd,grh->gdh", grouped_in, grouped_gate).astype(jnp.bfloat16).astype(jnp.float32)
        gate_grad = jnp.sum(gate_terms, axis=0).astype(jnp.bfloat16)
        gate_list.append(gate_grad.reshape(D, share_count, HID_DEV).transpose(1, 0, 2))
        running = jnp.zeros((block_count * CAP, D), jnp.float32)
        running_out = jnp.zeros((block_count * CAP, D), jnp.float32)
        for piece in range(share_count):
            lower = piece * HID_DEV
            upper = lower + HID_DEV
            partial_sum = jnp.dot(grad_gated[:, lower:upper], gate_full[:, lower:upper].T, preferred_element_type=jnp.float32)
            partial_sum = partial_sum + jnp.dot(grad_upper[:, lower:upper], up_full[:, lower:upper].T, preferred_element_type=jnp.float32)
            running = running + partial_sum.astype(jnp.bfloat16).astype(jnp.float32)
            out_part = jnp.dot(hidden_act[:, lower:upper], down_full[lower:upper, :], preferred_element_type=jnp.float32)
            running_out = running_out + out_part.astype(jnp.bfloat16).astype(jnp.float32)
        running = jnp.where(used_mask, running, 0.0)
        running_out = jnp.where(used_mask, router[:, None] * running_out, 0.0)
        grad_sum = grad_sum.at[row_index].add(running)
        out_sum = out_sum.at[row_index].add(running_out)
    grad_gate = jnp.concatenate(gate_list, axis=0)
    return out_sum.astype(jnp.bfloat16), grad_sum.astype(jnp.bfloat16), grad_gate
```

```python
import jax
import jax.numpy as jnp
from jax import lax
from jax.experimental import pallas as pl
from jax.experimental.pallas import tpu as pltpu
from jax.sharding import Mesh, PartitionSpec as P

EXPERTS = 8
CAP = 9
NZ = 8
AXES = ("z", "h", "y", "x", "c")
EP = ("y", "x", "c")
RIGHT = [(i, (i + 1) % NZ) for i in range(NZ)]
LEFT = [(i, (i - 1) % NZ) for i in range(NZ)]
SWAP = [(0, 1), (1, 0)]
BF = jnp.bfloat16
F32 = jnp.float32
VMEM_LIMIT = 60 * 1024 * 1024
ROWS = 288
D = 2048
HID = 768


def load_pieces(pieces, w_ref, sems):
    copies = [
        pltpu.make_async_copy(p, w_ref.at[pl.ds(i * 128, 128), :], sems.at[i])
        for i, p in enumerate(pieces)
    ]
    for c in copies:
        c.start()
    for c in copies:
        c.wait()


def hidden_kernel(x_ref, y_ref, *refs):
    pieces, h_ref, d_ref, gg, w_ref, sems = refs[:16], refs[16], refs[17], refs[18:34], refs[34], refs[35]
    load_pieces(pieces, w_ref, sems)
    x = x_ref[...]
    y = y_ref[...]
    for n in range(HID // 256):
        at = n * 256
        g = jnp.dot(x, w_ref[:, at : at + 256], preferred_element_type=F32)
        u = jnp.dot(x, w_ref[:, HID + at : HID + at + 256], preferred_element_type=F32)
        dh = jnp.dot(y, w_ref[:, 2 * HID + at : 2 * HID + at + 256], preferred_element_type=F32)
        s = 1.0 / (1.0 + jnp.exp(-g))
        gs = g * s
        h_ref[:, at : at + 256] = (gs * u).astype(BF)
        d_ref[:, HID + at : HID + at + 256] = (dh * gs).astype(BF)
        d_ref[:, at : at + 256] = (dh * u * s * (1.0 + g * (1.0 - s))).astype(BF)
    dg = d_ref[:, :HID]
    for i in range(16):
        gg[i][...] = lax.dot_general(
            x_ref[:, i * 128 : (i + 1) * 128], dg, (((0,), (0,)), ((), ())), preferred_element_type=F32
        ).astype(BF)


def rows_kernel(h_ref, d_ref, *refs):
    pieces, out_ref, back_ref, w_ref, sems = refs[:16], refs[16], refs[17], refs[18], refs[19]
    load_pieces(pieces, w_ref, sems)
    last = (((1,), (1,)), ((), ()))
    for n in range(D // 256):
        at = n * 256
        back_ref[:, at : at + 256] = lax.dot_general(
            d_ref[...], w_ref[at : at + 256, : 2 * HID], last, preferred_element_type=F32
        ).astype(BF)
        out_ref[:, at : at + 256] = lax.dot_general(
            h_ref[...], w_ref[at : at + 256, 2 * HID :], last, preferred_element_type=F32
        ).astype(BF)


VM = pl.BlockSpec(memory_space=pltpu.VMEM)
ANY = pl.BlockSpec(memory_space=pl.ANY)


def hidden_call(x, y, pieces):
    res = pl.pallas_call(
        hidden_kernel,
        out_shape=[
            jax.ShapeDtypeStruct((ROWS, HID), BF),
            jax.ShapeDtypeStruct((ROWS, 2 * HID), BF),
        ]
        + [jax.ShapeDtypeStruct((128, HID), BF)] * 16,
        in_specs=[VM, VM] + [ANY] * 16,
        out_specs=[VM] * 18,
        scratch_shapes=[pltpu.VMEM((D, 3 * HID), BF), pltpu.SemaphoreType.DMA((16,))],
        compiler_params=pltpu.CompilerParams(vmem_limit_bytes=VMEM_LIMIT),
        cost_estimate=pl.CostEstimate(flops=2 * ROWS * D * HID * 4, bytes_accessed=17_000_000, transcendentals=ROWS * HID),
    )(x, y, *pieces)
    return res[0], res[1], res[2:]


def rows_call(h, d, pieces):
    return pl.pallas_call(
        rows_kernel,
        out_shape=[jax.ShapeDtypeStruct((ROWS, D), BF)] * 2,
        in_specs=[VM, VM] + [ANY] * 16,
        out_specs=[VM] * 2,
        scratch_shapes=[pltpu.VMEM((D, 3 * HID), BF), pltpu.SemaphoreType.DMA((16,))],
        compiler_params=pltpu.CompilerParams(vmem_limit_bytes=VMEM_LIMIT),
        cost_estimate=pl.CostEstimate(flops=2 * ROWS * D * HID * 3, bytes_accessed=14_000_000, transcendentals=0),
    )(h, d, *pieces)


def right(v):
    return lax.ppermute(v, "z", RIGHT)


def left(v):
    return lax.ppermute(v, "z", LEFT)


def add(a, b):
    return (a.astype(F32) + b.astype(F32)).astype(BF)


def to_relative(v, z, h):
    rolled = lax.dynamic_slice(jnp.concatenate([v, v], axis=1), (0, z * 256), v.shape)
    parts = rolled.reshape(v.shape[0], NZ, 2, 128)
    return jnp.where(h == 1, parts[:, :, ::-1], parts).reshape(v.shape)


def from_relative(v, z, h):
    parts = v.reshape(v.shape[0], NZ, 2, 128)
    parts = jnp.where(h == 1, parts[:, :, ::-1], parts).reshape(v.shape)
    return lax.dynamic_slice(jnp.concatenate([parts, parts], axis=1), (0, (NZ - z) * 256), v.shape)


def per_device(tokens, grad_out, expert_ids, combine, w_gate, w_up, w_down):
    z, h = lax.axis_index("z"), lax.axis_index("h")
    own = jnp.concatenate([w_gate[0], w_up[0], w_down[0].T], axis=1)
    a, b = [None] * NZ, [None] * NZ
    a[0] = own
    b[0] = lax.ppermute(own, "h", SWAP)
    for s in range(1, 5):
        a[NZ - s] = right(a[(NZ - s + 1) % NZ])
        if s < 4:
            a[s] = left(a[s - 1])
    for s in range(1, 5):
        if s < 4:
            b[NZ - s] = right(b[(NZ - s + 1) % NZ])
        b[s] = left(b[s - 1])
    pieces = [v for pair in zip(a, b) for v in pair]

    e0, e1 = expert_ids[:, 0], expert_ids[:, 1]
    before = jnp.arange(32)[None, :] < jnp.arange(32)[:, None]

    def count(mine):
        hit = (e0[None, :] == mine[:, None]).astype(jnp.int32) + (e1[None, :] == mine[:, None]).astype(jnp.int32)
        return jnp.sum(jnp.where(before, hit, 0), axis=1)

    t0, t1 = e0 * CAP + count(e0), e1 * CAP + count(e1)
    slots = jnp.arange(EXPERTS * CAP, dtype=jnp.int32)[:, None]
    hit0, hit1 = slots == t0[None, :], slots == t1[None, :]
    pick = (hit0 | hit1).astype(BF)
    scale = jnp.sum(
        jnp.where(hit0, combine[:, 0][None, :], 0.0) + jnp.where(hit1, combine[:, 1][None, :], 0.0), axis=1
    )
    both = jnp.concatenate([to_relative(tokens, z, h), to_relative(grad_out, z, h)], axis=1)
    picked = jnp.dot(pick, both, preferred_element_type=F32)
    routed_x = picked[:, :D].astype(BF)
    routed_y = (picked[:, D:] * scale[:, None]).astype(BF)

    def fold(v, lead):
        return v.reshape(lead, CAP, 8, 256)

    payload = jnp.concatenate([fold(routed_x, EXPERTS), fold(routed_y, EXPERTS)], axis=1)
    payload = jnp.broadcast_to(payload[:, None], (EXPERTS, 4, 2 * CAP, 8, 256)).reshape(32, 2 * CAP, 8, 256)
    got = lax.all_to_all(payload, EP, 0, 0, tiled=True)
    x = got[:, :CAP].reshape(ROWS, D)
    y = got[:, CAP:].reshape(ROWS, D)

    hid, dgu, gg = hidden_call(x, y, pieces)

    mine, other = gg[0::2], gg[1::2]
    r, l = other[3], other[4]
    for s in range(1, 5):
        if s < 4:
            r = right(r)
            if s < 3:
                r = add(r, other[3 - s])
        l = left(l)
        if s < 4:
            l = add(l, other[4 + s])
    other_sum = (r.astype(F32) + l.astype(F32) + other[0].astype(F32)).astype(BF)
    crossed = lax.ppermute(other_sum, "h", SWAP)
    r, l = mine[4], mine[5]
    for s in range(1, 5):
        r = right(r)
        if s < 4:
            r = add(r, mine[4 - s])
            l = left(l)
            if s < 3:
                l = add(l, mine[5 + s])
    grad_gate = (r.astype(F32) + l.astype(F32) + mine[0].astype(F32) + crossed.astype(F32)).astype(BF)[None]

    out_rows, back_rows = rows_call(hid, dgu, pieces)
    payload = jnp.concatenate([fold(out_rows, 32), fold(back_rows, 32)], axis=1)
    got = lax.all_to_all(payload, EP, 0, 0, tiled=True)
    total = jnp.sum(got.reshape(EXPERTS, 4, 2 * CAP, 8, 256).astype(F32), axis=1)
    sum_out = total[:, :CAP].reshape(EXPERTS * CAP, D) * scale[:, None]
    sum_back = total[:, CAP:].reshape(EXPERTS * CAP, D)
    place = (hit0 | hit1).astype(F32)
    back = lax.dot_general(
        place,
        jnp.concatenate([sum_out, sum_back], axis=1),
        (((0,), (0,)), ((), ())),
        precision=lax.Precision.HIGHEST,
        preferred_element_type=F32,
    ).astype(BF)
    layer_out = from_relative(back[:, :D], z, h)
    grad_tokens = from_relative(back[:, D:], z, h)
    return (layer_out, grad_tokens, grad_gate)


def solution(mesh):
    fine = Mesh(mesh.devices.reshape(NZ, 2, 4, 4, 2), AXES)
    dp = ("z", "h")
    placed = (
        P(AXES, None),
        P(AXES, None),
        P(AXES, None),
        P(AXES, None),
        P(EP, dp, None),
        P(EP, dp, None),
        P(EP, None, dp),
    )
    return jax.shard_map(
        per_device,
        mesh=fine,
        in_specs=placed,
        out_specs=(P(AXES, None), P(AXES, None), P(EP, dp, None)),
        check_vma=False,
    )
```

```python
import jax
import jax.numpy as jnp
from jax import lax
from jax.experimental import pallas as pl
from jax.experimental.pallas import tpu as pltpu
from jax.sharding import Mesh, PartitionSpec as P

EXPERTS = 8
CAP = 9
NZ = 8
AXES = ("z", "h", "y", "e", "l", "c")
EP = ("y", "e", "l", "c")
GROUP = ("y", "e")
RIGHT = [(i, (i + 1) % NZ) for i in range(NZ)]
LEFT = [(i, (i - 1) % NZ) for i in range(NZ)]
SWAP = [(0, 1), (1, 0)]
BF = jnp.bfloat16
F32 = jnp.float32
VMEM_LIMIT = 8 * 1024 * 1024
ORDER = (0, 1, 7, 2, 6, 3, 5, 4)
PLACE = tuple(ORDER.index(k) for k in range(NZ))
ROWS = 288
D = 2048
HID = 768


HALF = D // 2
PARTIAL_FLOPS = 30_000_000_000


def pair(pieces, p, at, width):
    return jnp.concatenate([pieces[2 * p][:, at : at + width], pieces[2 * p + 1][:, at : at + width]], axis=0)


def half_dot(v_ref, start, pieces, at):
    acc = None
    for p in range(NZ // 2):
        left = start + p * 256
        term = jnp.dot(v_ref[:, left : left + 256], pair(pieces, p, at, 256), preferred_element_type=F32)
        acc = term if acc is None else acc + term
    return acc


def partial_kernel(x_ref, y_ref, *refs):
    pieces, acc_ref = refs[:NZ], refs[NZ]
    for m in range(3 * HID // 256):
        at = m * 256
        acc_ref[:, at : at + 256] = half_dot(x_ref if m < 6 else y_ref, 0, pieces, at)


def hidden_kernel(x_ref, y_ref, acc_ref, *refs):
    pieces = refs[:16]
    keep_ref, send_ref, d_ref, h_ref = refs[16:]

    def pre(v_ref, at):
        return acc_ref[:, at : at + 256] + half_dot(v_ref, HALF, pieces[NZ:], at)

    for m in range(HID // 256):
        at = m * 256
        g = pre(x_ref, at)
        u = pre(x_ref, HID + at)
        dh = pre(y_ref, 2 * HID + at)
        s = 1.0 / (1.0 + jnp.exp(-g))
        gs = g * s
        h_ref[:, at : at + 256] = (gs * u).astype(BF)
        d_ref[:, HID + at : HID + at + 256] = (dh * gs).astype(BF)
        d_ref[:, at : at + 256] = (dh * u * s * (1.0 + g * (1.0 - s))).astype(BF)
    last = (((1,), (1,)), ((), ()))
    half = ROWS // 2
    for p in range(NZ):
        at = p * 256
        out = lax.dot_general(h_ref[...], pair(pieces, p, 2 * HID, HID), last, preferred_element_type=F32)
        back = lax.dot_general(d_ref[...], pair(pieces, p, 0, 2 * HID), last, preferred_element_type=F32)
        for j, v in enumerate((out, back)):
            keep_ref[j, :, at : at + 256] = v[:half].astype(BF)
            send_ref[j, :, at : at + 256] = v[half:].astype(BF)


def gate_kernel(x_ref, d_ref, *gg):
    dg = d_ref[:, :HID]
    for p in range(NZ):
        for g in range(2):
            at = g * HALF + p * 128
            gg[p][g * 128 : (g + 1) * 128, :] = lax.dot_general(
                x_ref[:, at : at + 128], dg, (((0,), (0,)), ((), ())), preferred_element_type=F32
            ).astype(BF)


VM = pl.BlockSpec(memory_space=pltpu.VMEM)


def params():
    return pltpu.CompilerParams(vmem_limit_bytes=VMEM_LIMIT)


def cost(flops, size):
    return pl.CostEstimate(flops=flops, bytes_accessed=size, transcendentals=0)


def partial_call(x, y, pieces):
    return pl.pallas_call(
        partial_kernel,
        out_shape=jax.ShapeDtypeStruct((ROWS, 3 * HID), F32),
        in_specs=[VM] * (2 + NZ),
        out_specs=VM,
        compiler_params=params(),
        cost_estimate=cost(PARTIAL_FLOPS, 10_000_000),
    )(x, y, *pieces)


def hidden_call(x, y, acc, pieces):
    return pl.pallas_call(
        hidden_kernel,
        out_shape=[jax.ShapeDtypeStruct((2, ROWS // 2, D), BF)] * 2 + [jax.ShapeDtypeStruct((ROWS, 2 * HID), BF)],
        in_specs=[VM] * 19,
        out_specs=[VM] * 3,
        scratch_shapes=[pltpu.VMEM((ROWS, HID), BF)],
        compiler_params=params(),
        cost_estimate=cost(2 * ROWS * D * HID * 3, 20_000_000),
    )(x, y, acc, *pieces)


def gate_call(x, d):
    return pl.pallas_call(
        gate_kernel,
        out_shape=[jax.ShapeDtypeStruct((256, HID), BF)] * NZ,
        in_specs=[VM] * 2,
        out_specs=[VM] * NZ,
        compiler_params=params(),
        cost_estimate=cost(2 * ROWS * D * HID, 6_000_000),
    )(x, d)


def right(v):
    return lax.ppermute(v, "z", RIGHT)


def left(v):
    return lax.ppermute(v, "z", LEFT)


def add(a, b):
    return (a.astype(F32) + b.astype(F32)).astype(BF)


def to_relative(v, z, h):
    rolled = lax.dynamic_slice(jnp.concatenate([v, v], axis=1), (0, z * 256), v.shape)
    even, odd = (
        jnp.concatenate([rolled[:, k * 256 + g * 128 : k * 256 + g * 128 + 128] for k in ORDER], axis=1)
        for g in range(2)
    )
    return jnp.concatenate([jnp.where(h == 0, even, odd), jnp.where(h == 0, odd, even)], axis=1)


def from_relative(v, z, h):
    even = jnp.where(h == 0, v[:, :HALF], v[:, HALF:])
    odd = jnp.where(h == 0, v[:, HALF:], v[:, :HALF])
    parts = jnp.concatenate([t[:, p * 128 : p * 128 + 128] for p in PLACE for t in (even, odd)], axis=1)
    return lax.dynamic_slice(jnp.concatenate([parts, parts], axis=1), (0, (NZ - z) * 256), v.shape)


def per_device(tokens, grad_out, expert_ids, combine, w_gate, w_up, w_down):
    z, h = lax.axis_index("z"), lax.axis_index("h")
    own = jnp.concatenate([w_gate[0], w_up[0], w_down[0].T], axis=1)
    a, b = [None] * NZ, [None] * NZ
    b[0] = lax.ppermute(own, "h", SWAP)
    both = jnp.concatenate([to_relative(tokens, z, h), to_relative(grad_out, z, h)], axis=1)
    e0, e1 = expert_ids[:, 0], expert_ids[:, 1]
    before = jnp.arange(32)[None, :] < jnp.arange(32)[:, None]

    def count(mine):
        hit = (e0[None, :] == mine[:, None]).astype(jnp.int32) + (e1[None, :] == mine[:, None]).astype(jnp.int32)
        return jnp.sum(jnp.where(before, hit, 0), axis=1)

    t0, t1 = e0 * CAP + count(e0), e1 * CAP + count(e1)
    slots = jnp.arange(EXPERTS * CAP, dtype=jnp.int32)[:, None]
    hit0, hit1 = slots == t0[None, :], slots == t1[None, :]
    pick = (hit0 | hit1).astype(BF)
    scale = jnp.sum(
        jnp.where(hit0, combine[:, 0][None, :], 0.0) + jnp.where(hit1, combine[:, 1][None, :], 0.0), axis=1
    )
    picked = jnp.dot(pick, both, preferred_element_type=F32)
    a[0] = own
    for s in range(1, 5):
        a[NZ - s] = right(a[(NZ - s + 1) % NZ])
        if s < 4:
            a[s] = left(a[s - 1])
    for s in range(1, 5):
        if s < 4:
            b[NZ - s] = right(b[(NZ - s + 1) % NZ])
        b[s] = left(b[s - 1])
    mine = [a[k] for k in ORDER]
    pieces = mine + [b[k] for k in ORDER]

    routed_x = picked[:, :D].astype(BF)
    routed_y = (picked[:, D:] * scale[:, None]).astype(BF)

    def fold(v, lead):
        return v.reshape(lead, CAP, 8, 256)

    payload = jnp.concatenate([fold(routed_x, EXPERTS), fold(routed_y, EXPERTS)], axis=1)
    block = lax.all_to_all(payload, GROUP, 0, 0, tiled=True)
    beside = lax.ppermute(block, "l", SWAP)
    quarters = (block, beside, lax.ppermute(block, "c", SWAP), lax.ppermute(beside, "c", SWAP))
    x = jnp.concatenate([q[:, :CAP].reshape(ROWS // 4, D) for q in quarters], axis=0)
    y = jnp.concatenate([q[:, CAP:].reshape(ROWS // 4, D) for q in quarters], axis=0)

    acc = partial_call(x, y, mine)
    keep, send, dgu = hidden_call(x, y, acc, pieces)
    gg = gate_call(x, dgu)
    crossed = lax.ppermute(send, "c", SWAP)
    quarter = (keep.astype(F32) + crossed.astype(F32)).astype(BF).reshape(2, 2, 72, D)
    summed = add(quarter[:, 0], lax.ppermute(quarter[:, 1], "l", SWAP))
    payload = jnp.concatenate([fold(summed[0], EXPERTS), fold(summed[1], EXPERTS)], axis=1)
    got = lax.all_to_all(payload, GROUP, 0, 0, tiled=True)

    gg = [gg[p] for p in PLACE]
    r, l = gg[4], gg[5]
    for s in range(1, 5):
        r = right(r)
        if s < 4:
            r = add(r, gg[4 - s])
            l = left(l)
            if s < 3:
                l = add(l, gg[5 + s])
    near = r.astype(F32) + l.astype(F32) + gg[0].astype(F32)
    crossed = lax.ppermute(near[128:].astype(BF), "h", SWAP)
    grad_gate = (near[:128] + crossed.astype(F32)).astype(BF)[None]

    total = got.astype(F32)
    sum_out = total[:, :CAP].reshape(EXPERTS * CAP, D) * scale[:, None]
    sum_back = total[:, CAP:].reshape(EXPERTS * CAP, D)
    place = (hit0 | hit1).astype(F32)
    back = lax.dot_general(
        place,
        jnp.concatenate([sum_out, sum_back], axis=1),
        (((0,), (0,)), ((), ())),
        precision=lax.Precision.HIGHEST,
        preferred_element_type=F32,
    ).astype(BF)
    layer_out = from_relative(back[:, :D], z, h)
    grad_tokens = from_relative(back[:, D:], z, h)
    return (layer_out, grad_tokens, grad_gate)


def solution(mesh):
    fine = Mesh(mesh.devices.reshape(NZ, 2, 4, 2, 2, 2), AXES)
    dp = ("z", "h")
    placed = (
        P(AXES, None),
        P(AXES, None),
        P(AXES, None),
        P(AXES, None),
        P(EP, dp, None),
        P(EP, dp, None),
        P(EP, None, dp),
    )
    return jax.shard_map(
        per_device,
        mesh=fine,
        in_specs=placed,
        out_specs=(P(AXES, None), P(AXES, None), P(EP, dp, None)),
        check_vma=False,
    )
```

```python
import jax
import jax.numpy as jnp
from jax import lax
from jax.experimental import pallas as pl
from jax.experimental.pallas import tpu as pltpu
from jax.sharding import Mesh, PartitionSpec as P

EXPERTS = 8
CAP = 9
NZ = 8
AXES = ("z", "h", "y", "e", "l", "c")
EP = ("y", "e", "l", "c")
GROUP = ("y", "e")
RIGHT = [(i, (i + 1) % NZ) for i in range(NZ)]
LEFT = [(i, (i - 1) % NZ) for i in range(NZ)]
SWAP = [(0, 1), (1, 0)]
BF = jnp.bfloat16
F32 = jnp.float32
VMEM_LIMIT = 8 * 1024 * 1024
ORDER = (0, 1, 7, 2, 6, 3, 5, 4)
PLACE = tuple(ORDER.index(k) for k in range(NZ))
ROWS = 288
D = 2048
HID = 768


HALF = D // 2
PARTIAL_FLOPS = 5_000_000_000


def pair(pieces, p, at, width):
    return jnp.concatenate([pieces[2 * p][:, at : at + width], pieces[2 * p + 1][:, at : at + width]], axis=0)


def half_dot(v_ref, start, pieces, at):
    acc = None
    for p in range(NZ // 2):
        left = start + p * 256
        term = jnp.dot(v_ref[:, left : left + 256], pair(pieces, p, at, 256), preferred_element_type=F32)
        acc = term if acc is None else acc + term
    return acc


def partial_kernel(x_ref, y_ref, *refs):
    pieces, acc_ref = refs[:NZ], refs[NZ]
    for m in range(3 * HID // 256):
        at = m * 256
        acc_ref[:, at : at + 256] = half_dot(x_ref if m < 6 else y_ref, 0, pieces, at)


def hidden_kernel(x_ref, y_ref, acc_ref, *refs):
    pieces = refs[:16]
    keep_ref, send_ref, d_ref, h_ref = refs[16:]

    def pre(v_ref, at):
        return acc_ref[:, at : at + 256] + half_dot(v_ref, HALF, pieces[NZ:], at)

    for m in range(HID // 256):
        at = m * 256
        g = pre(x_ref, at)
        u = pre(x_ref, HID + at)
        dh = pre(y_ref, 2 * HID + at)
        s = 1.0 / (1.0 + jnp.exp(-g))
        gs = g * s
        h_ref[:, at : at + 256] = (gs * u).astype(BF)
        d_ref[:, HID + at : HID + at + 256] = (dh * gs).astype(BF)
        d_ref[:, at : at + 256] = (dh * u * s * (1.0 + g * (1.0 - s))).astype(BF)
    last = (((1,), (1,)), ((), ()))
    half = ROWS // 2
    for p in range(NZ):
        at = p * 256
        out = lax.dot_general(h_ref[...], pair(pieces, p, 2 * HID, HID), last, preferred_element_type=F32)
        back = lax.dot_general(d_ref[...], pair(pieces, p, 0, 2 * HID), last, preferred_element_type=F32)
        for j, v in enumerate((out, back)):
            keep_ref[j, :, at : at + 256] = v[:half].astype(BF)
            send_ref[j, :, at : at + 256] = v[half:].astype(BF)


def gate_kernel(x_ref, d_ref, *gg):
    dg = d_ref[:, :HID]
    for p in range(NZ):
        for g in range(2):
            at = g * HALF + p * 128
            gg[p][g * 128 : (g + 1) * 128, :] = lax.dot_general(
                x_ref[:, at : at + 128], dg, (((0,), (0,)), ((), ())), preferred_element_type=F32
            ).astype(BF)


VM = pl.BlockSpec(memory_space=pltpu.VMEM)


def params():
    return pltpu.CompilerParams(vmem_limit_bytes=VMEM_LIMIT)


def cost(flops, size):
    return pl.CostEstimate(flops=flops, bytes_accessed=size, transcendentals=0)


def partial_call(x, y, pieces):
    return pl.pallas_call(
        partial_kernel,
        out_shape=jax.ShapeDtypeStruct((ROWS, 3 * HID), F32),
        in_specs=[VM] * (2 + NZ),
        out_specs=VM,
        compiler_params=params(),
        cost_estimate=cost(PARTIAL_FLOPS, 10_000_000),
    )(x, y, *pieces)


def hidden_call(x, y, acc, pieces):
    return pl.pallas_call(
        hidden_kernel,
        out_shape=[jax.ShapeDtypeStruct((2, ROWS // 2, D), BF)] * 2 + [jax.ShapeDtypeStruct((ROWS, 2 * HID), BF)],
        in_specs=[VM] * 19,
        out_specs=[VM] * 3,
        scratch_shapes=[pltpu.VMEM((ROWS, HID), BF)],
        compiler_params=params(),
        cost_estimate=cost(2 * ROWS * D * HID * 3, 20_000_000),
    )(x, y, acc, *pieces)


def gate_call(x, d):
    return pl.pallas_call(
        gate_kernel,
        out_shape=[jax.ShapeDtypeStruct((256, HID), BF)] * NZ,
        in_specs=[VM] * 2,
        out_specs=[VM] * NZ,
        compiler_params=params(),
        cost_estimate=cost(2 * ROWS * D * HID, 6_000_000),
    )(x, d)


def right(v):
    return lax.ppermute(v, "z", RIGHT)


def left(v):
    return lax.ppermute(v, "z", LEFT)


def add(a, b):
    return (a.astype(F32) + b.astype(F32)).astype(BF)


def to_relative(v, z, h):
    rolled = lax.dynamic_slice(jnp.concatenate([v, v], axis=1), (0, z * 256), v.shape)
    even, odd = (
        jnp.concatenate([rolled[:, k * 256 + g * 128 : k * 256 + g * 128 + 128] for k in ORDER], axis=1)
        for g in range(2)
    )
    return jnp.concatenate([jnp.where(h == 0, even, odd), jnp.where(h == 0, odd, even)], axis=1)


def from_relative(v, z, h):
    even = jnp.where(h == 0, v[:, :HALF], v[:, HALF:])
    odd = jnp.where(h == 0, v[:, HALF:], v[:, :HALF])
    parts = jnp.concatenate([t[:, p * 128 : p * 128 + 128] for p in PLACE for t in (even, odd)], axis=1)
    return lax.dynamic_slice(jnp.concatenate([parts, parts], axis=1), (0, (NZ - z) * 256), v.shape)


def per_device(tokens, grad_out, expert_ids, combine, w_gate, w_up, w_down):
    z, h = lax.axis_index("z"), lax.axis_index("h")
    own = jnp.concatenate([w_gate[0], w_up[0], w_down[0].T], axis=1)
    a, b = [None] * NZ, [None] * NZ
    b[0] = lax.ppermute(own, "h", SWAP)
    both = jnp.concatenate([to_relative(tokens, z, h), to_relative(grad_out, z, h)], axis=1)
    e0, e1 = expert_ids[:, 0], expert_ids[:, 1]
    before = jnp.arange(32)[None, :] < jnp.arange(32)[:, None]

    def count(mine):
        hit = (e0[None, :] == mine[:, None]).astype(jnp.int32) + (e1[None, :] == mine[:, None]).astype(jnp.int32)
        return jnp.sum(jnp.where(before, hit, 0), axis=1)

    t0, t1 = e0 * CAP + count(e0), e1 * CAP + count(e1)
    slots = jnp.arange(EXPERTS * CAP, dtype=jnp.int32)[:, None]
    hit0, hit1 = slots == t0[None, :], slots == t1[None, :]
    pick = (hit0 | hit1).astype(BF)
    scale = jnp.sum(
        jnp.where(hit0, combine[:, 0][None, :], 0.0) + jnp.where(hit1, combine[:, 1][None, :], 0.0), axis=1
    )
    picked = jnp.dot(pick, both, preferred_element_type=F32)
    a[0] = own
    routed_x = picked[:, :D].astype(BF)
    routed_y = (picked[:, D:] * scale[:, None]).astype(BF)

    def fold(v, lead):
        return v.reshape(lead, CAP, 8, 256)

    payload = jnp.concatenate([fold(routed_x, EXPERTS), fold(routed_y, EXPERTS)], axis=1)
    for s in range(1, 5):
        a[NZ - s] = right(a[(NZ - s + 1) % NZ])
        if s < 4:
            a[s] = left(a[s - 1])
        if s == 2:
            payload, b[0], a[2], a[6] = lax.optimization_barrier((payload, b[0], a[2], a[6]))
    for s in range(1, 5):
        if s < 4:
            b[NZ - s] = right(b[(NZ - s + 1) % NZ])
        b[s] = left(b[s - 1])
    mine = [a[k] for k in ORDER]
    pieces = mine + [b[k] for k in ORDER]
    block = lax.all_to_all(payload, GROUP, 0, 0, tiled=True)
    beside = lax.ppermute(block, "l", SWAP)
    quarters = (block, beside, lax.ppermute(block, "c", SWAP), lax.ppermute(beside, "c", SWAP))
    x = jnp.concatenate([q[:, :CAP].reshape(ROWS // 4, D) for q in quarters], axis=0)
    y = jnp.concatenate([q[:, CAP:].reshape(ROWS // 4, D) for q in quarters], axis=0)

    acc = partial_call(x, y, mine)
    keep, send, dgu = hidden_call(x, y, acc, pieces)
    gg = gate_call(x, dgu)
    crossed = lax.ppermute(send, "c", SWAP)
    quarter = (keep.astype(F32) + crossed.astype(F32)).astype(BF).reshape(2, 2, 72, D)
    summed = add(quarter[:, 0], lax.ppermute(quarter[:, 1], "l", SWAP))
    payload = jnp.concatenate([fold(summed[0], EXPERTS), fold(summed[1], EXPERTS)], axis=1)
    got = lax.all_to_all(payload, GROUP, 0, 0, tiled=True)

    gg = [gg[p] for p in PLACE]
    r, l = gg[4], gg[5]
    for s in range(1, 5):
        r = right(r)
        if s < 4:
            r = add(r, gg[4 - s])
            l = left(l)
            if s < 3:
                l = add(l, gg[5 + s])
    near = r.astype(F32) + l.astype(F32) + gg[0].astype(F32)
    crossed = lax.ppermute(near[128:].astype(BF), "h", SWAP)
    grad_gate = (near[:128] + crossed.astype(F32)).astype(BF)[None]

    total = got.astype(F32)
    sum_out = total[:, :CAP].reshape(EXPERTS * CAP, D) * scale[:, None]
    sum_back = total[:, CAP:].reshape(EXPERTS * CAP, D)
    place = (hit0 | hit1).astype(F32)
    back = lax.dot_general(
        place,
        jnp.concatenate([sum_out, sum_back], axis=1),
        (((0,), (0,)), ((), ())),
        precision=lax.Precision.HIGHEST,
        preferred_element_type=F32,
    ).astype(BF)
    layer_out = from_relative(back[:, :D], z, h)
    grad_tokens = from_relative(back[:, D:], z, h)
    return (layer_out, grad_tokens, grad_gate)


def solution(mesh):
    fine = Mesh(mesh.devices.reshape(NZ, 2, 4, 2, 2, 2), AXES)
    dp = ("z", "h")
    placed = (
        P(AXES, None),
        P(AXES, None),
        P(AXES, None),
        P(AXES, None),
        P(EP, dp, None),
        P(EP, dp, None),
        P(EP, None, dp),
    )
    return jax.shard_map(
        per_device,
        mesh=fine,
        in_specs=placed,
        out_specs=(P(AXES, None), P(AXES, None), P(EP, dp, None)),
        check_vma=False,
    )
```

```python
import jax
import jax.numpy as jnp
from jax import lax
from jax.experimental import pallas as pl
from jax.experimental.pallas import tpu as pltpu
from jax.sharding import Mesh, PartitionSpec as P

EXPERTS = 8
CAP = 9
NZ = 8
AXES = ("z", "h", "y", "e", "l", "c")
EP = ("y", "e", "l", "c")
GROUP = ("y", "e")
RIGHT = [(i, (i + 1) % NZ) for i in range(NZ)]
LEFT = [(i, (i - 1) % NZ) for i in range(NZ)]
SWAP = [(0, 1), (1, 0)]
BF = jnp.bfloat16
F32 = jnp.float32
VMEM_LIMIT = 8 * 1024 * 1024
ORDER = (0, 1, 7, 2, 6, 3, 5, 4)
PLACE = tuple(ORDER.index(k) for k in range(NZ))
ROWS = 288
D = 2048
HID = 768


HALF = D // 2
PARTIAL_FLOPS = 5_000_000_000


def pair(pieces, p, at, width):
    return jnp.concatenate([pieces[2 * p][:, at : at + width], pieces[2 * p + 1][:, at : at + width]], axis=0)


def half_dot(v_ref, start, pieces, at):
    acc = None
    for p in range(NZ // 2):
        left = start + p * 256
        term = jnp.dot(v_ref[:, left : left + 256], pair(pieces, p, at, 256), preferred_element_type=F32)
        acc = term if acc is None else acc + term
    return acc


def partial_kernel(x_ref, y_ref, *refs):
    pieces, acc_ref = refs[:NZ], refs[NZ]
    for m in range(3 * HID // 256):
        at = m * 256
        acc_ref[:, at : at + 256] = half_dot(x_ref if m < 6 else y_ref, 0, pieces, at)


def hidden_kernel(x_ref, y_ref, acc_ref, *refs):
    pieces = refs[:16]
    keep_ref, send_ref, d_ref, h_ref = refs[16:]

    def pre(v_ref, at):
        return acc_ref[:, at : at + 256] + half_dot(v_ref, HALF, pieces[NZ:], at)

    for m in range(HID // 256):
        at = m * 256
        g = pre(x_ref, at)
        u = pre(x_ref, HID + at)
        dh = pre(y_ref, 2 * HID + at)
        s = 1.0 / (1.0 + jnp.exp(-g))
        gs = g * s
        h_ref[:, at : at + 256] = (gs * u).astype(BF)
        d_ref[:, HID + at : HID + at + 256] = (dh * gs).astype(BF)
        d_ref[:, at : at + 256] = (dh * u * s * (1.0 + g * (1.0 - s))).astype(BF)
    last = (((1,), (1,)), ((), ()))
    half = ROWS // 2
    for p in range(NZ):
        at = p * 256
        out = lax.dot_general(h_ref[...], pair(pieces, p, 2 * HID, HID), last, preferred_element_type=F32)
        back = lax.dot_general(d_ref[...], pair(pieces, p, 0, 2 * HID), last, preferred_element_type=F32)
        for j, v in enumerate((out, back)):
            keep_ref[j, :, at : at + 256] = v[:half].astype(BF)
            send_ref[j, :, at : at + 256] = v[half:].astype(BF)


def gate_kernel(x_ref, d_ref, *gg):
    dg = d_ref[:, :HID]
    for p in range(NZ):
        for g in range(2):
            at = g * HALF + p * 128
            gg[p][g * 128 : (g + 1) * 128, :] = lax.dot_general(
                x_ref[:, at : at + 128], dg, (((0,), (0,)), ((), ())), preferred_element_type=F32
            ).astype(BF)


VM = pl.BlockSpec(memory_space=pltpu.VMEM)


def params():
    return pltpu.CompilerParams(vmem_limit_bytes=VMEM_LIMIT)


def cost(flops, size):
    return pl.CostEstimate(flops=flops, bytes_accessed=size, transcendentals=0)


def partial_call(x, y, pieces):
    return pl.pallas_call(
        partial_kernel,
        out_shape=jax.ShapeDtypeStruct((ROWS, 3 * HID), F32),
        in_specs=[VM] * (2 + NZ),
        out_specs=VM,
        compiler_params=params(),
        cost_estimate=cost(PARTIAL_FLOPS, 10_000_000),
    )(x, y, *pieces)


def hidden_call(x, y, acc, pieces):
    return pl.pallas_call(
        hidden_kernel,
        out_shape=[jax.ShapeDtypeStruct((2, ROWS // 2, D), BF)] * 2 + [jax.ShapeDtypeStruct((ROWS, 2 * HID), BF)],
        in_specs=[VM] * 19,
        out_specs=[VM] * 3,
        scratch_shapes=[pltpu.VMEM((ROWS, HID), BF)],
        compiler_params=params(),
        cost_estimate=cost(2 * ROWS * D * HID * 3, 20_000_000),
    )(x, y, acc, *pieces)


def gate_call(x, d):
    return pl.pallas_call(
        gate_kernel,
        out_shape=[jax.ShapeDtypeStruct((256, HID), BF)] * NZ,
        in_specs=[VM] * 2,
        out_specs=[VM] * NZ,
        compiler_params=params(),
        cost_estimate=cost(2 * ROWS * D * HID, 6_000_000),
    )(x, d)


def right(v):
    return lax.ppermute(v, "z", RIGHT)


def left(v):
    return lax.ppermute(v, "z", LEFT)


def add(a, b):
    return (a.astype(F32) + b.astype(F32)).astype(BF)


def to_relative(v, z, h):
    rolled = lax.dynamic_slice(jnp.concatenate([v, v], axis=1), (0, z * 256), v.shape)
    even, odd = (
        jnp.concatenate([rolled[:, k * 256 + g * 128 : k * 256 + g * 128 + 128] for k in ORDER], axis=1)
        for g in range(2)
    )
    return jnp.concatenate([jnp.where(h == 0, even, odd), jnp.where(h == 0, odd, even)], axis=1)


def from_relative(v, z, h):
    even = jnp.where(h == 0, v[:, :HALF], v[:, HALF:])
    odd = jnp.where(h == 0, v[:, HALF:], v[:, :HALF])
    parts = jnp.concatenate([t[:, p * 128 : p * 128 + 128] for p in PLACE for t in (even, odd)], axis=1)
    return lax.dynamic_slice(jnp.concatenate([parts, parts], axis=1), (0, (NZ - z) * 256), v.shape)


def per_device(tokens, grad_out, expert_ids, combine, w_gate, w_up, w_down):
    z, h = lax.axis_index("z"), lax.axis_index("h")
    own = jnp.concatenate([w_gate[0], w_up[0], w_down[0].T], axis=1)
    a, b = [None] * NZ, [None] * NZ
    b[0] = lax.ppermute(own, "h", SWAP)
    both = jnp.concatenate([to_relative(tokens, z, h), to_relative(grad_out, z, h)], axis=1)
    e0, e1 = expert_ids[:, 0], expert_ids[:, 1]
    before = jnp.arange(32)[None, :] < jnp.arange(32)[:, None]

    def count(mine):
        hit = (e0[None, :] == mine[:, None]).astype(jnp.int32) + (e1[None, :] == mine[:, None]).astype(jnp.int32)
        return jnp.sum(jnp.where(before, hit, 0), axis=1)

    t0, t1 = e0 * CAP + count(e0), e1 * CAP + count(e1)
    slots = jnp.arange(EXPERTS * CAP, dtype=jnp.int32)[:, None]
    hit0, hit1 = slots == t0[None, :], slots == t1[None, :]
    pick = (hit0 | hit1).astype(BF)
    scale = jnp.sum(
        jnp.where(hit0, combine[:, 0][None, :], 0.0) + jnp.where(hit1, combine[:, 1][None, :], 0.0), axis=1
    )
    picked = jnp.dot(pick, both, preferred_element_type=F32)
    a[0] = own
    routed_x = picked[:, :D].astype(BF)
    routed_y = (picked[:, D:] * scale[:, None]).astype(BF)

    def fold(v, lead):
        return v.reshape(lead, CAP, 8, 256)

    payload = jnp.concatenate([fold(routed_x, EXPERTS), fold(routed_y, EXPERTS)], axis=1)
    for s in range(1, 5):
        a[NZ - s] = right(a[(NZ - s + 1) % NZ])
        if s < 4:
            a[s] = left(a[s - 1])
        if s == 2:
            payload, b[0], a[2], a[6] = lax.optimization_barrier((payload, b[0], a[2], a[6]))
    for s in range(1, 5):
        if s < 4:
            b[NZ - s] = right(b[(NZ - s + 1) % NZ])
        b[s] = left(b[s - 1])
    mine = [a[k] for k in ORDER]
    pieces = mine + [b[k] for k in ORDER]
    block = lax.all_to_all(payload, GROUP, 0, 0, tiled=True)
    beside = lax.ppermute(block, "l", SWAP)
    quarters = (block, beside, lax.ppermute(block, "c", SWAP), lax.ppermute(beside, "c", SWAP))
    x = jnp.concatenate([q[:, :CAP].reshape(ROWS // 4, D) for q in quarters], axis=0)
    y = jnp.concatenate([q[:, CAP:].reshape(ROWS // 4, D) for q in quarters], axis=0)

    acc = partial_call(x, y, mine)
    keep, send, dgu = hidden_call(x, y, acc, pieces)
    gg = gate_call(x, dgu)
    crossed = lax.ppermute(send, "c", SWAP)
    quarter = (keep.astype(F32) + crossed.astype(F32)).astype(BF).reshape(2, 2, 72, D)
    summed = add(quarter[:, 0], lax.ppermute(quarter[:, 1], "l", SWAP))
    payload = jnp.concatenate([fold(summed[0], EXPERTS), fold(summed[1], EXPERTS)], axis=1)
    got = lax.all_to_all(payload, GROUP, 0, 0, tiled=True)

    gg = [gg[p] for p in PLACE]
    r, l = gg[4], gg[5]
    for s in range(1, 5):
        r = right(r)
        if s < 4:
            r = add(r, gg[4 - s])
            l = left(l)
            if s < 3:
                l = add(l, gg[5 + s])
    near = r.astype(F32) + l.astype(F32) + gg[0].astype(F32)
    crossed = lax.ppermute(near[128:].astype(BF), "h", SWAP)
    grad_gate = (near[:128] + crossed.astype(F32)).astype(BF)[None]

    def combined(rows, **kw):
        spread = (hit0 | hit1).astype(rows.dtype)
        return lax.dot_general(spread, rows, (((0,), (0,)), ((), ())), preferred_element_type=F32, **kw).astype(BF)

    sum_out = got[:, :CAP].astype(F32).reshape(EXPERTS * CAP, D) * scale[:, None]
    layer_out = from_relative(combined(sum_out, precision=lax.Precision.HIGHEST), z, h)
    grad_tokens = from_relative(combined(got[:, CAP:].reshape(EXPERTS * CAP, D)), z, h)
    return (layer_out, grad_tokens, grad_gate)


def solution(mesh):
    fine = Mesh(mesh.devices.reshape(NZ, 2, 4, 2, 2, 2), AXES)
    dp = ("z", "h")
    placed = (
        P(AXES, None),
        P(AXES, None),
        P(AXES, None),
        P(AXES, None),
        P(EP, dp, None),
        P(EP, dp, None),
        P(EP, None, dp),
    )
    return jax.shard_map(
        per_device,
        mesh=fine,
        in_specs=placed,
        out_specs=(P(AXES, None), P(AXES, None), P(EP, dp, None)),
        check_vma=False,
    )
```
